512 devices in a mesh: amp: 64 (over y, z), int: 8 (over x, core).
Axes of the slice: x: 4, y: 4, z: 16, core: 2. Of those that a mesh axis runs over, the one named last changes fastest.
Arguments:
- amps: bfloat16 [512, 1024, 128], P('amp', 'int'), may hold values from -6 to 6
- integrals: bfloat16 [512, 16, 128, 128], P('amp', 'int'), may hold values from -0.125 to 0.125
- hole_int: bfloat16 [1024, 1024], replicated, may hold values from -0.1875 to 0.1875
- send_list: int32 [64, 64, 1], P('amp'), may hold values from 0 to 7, as said below
- slot_of: int32 [512, 16], P('amp'), may hold values from 0 to 63, as said below
Outputs:
- residual: bfloat16 [512, 1024, 128], P('amp', 'int')
The draws below stay inside these ranges and needn't reach their ends.
Inputs may be any that keep to these rules, and one draw needn't show every extreme that they name: `send_list`: every local tile index appears in each source device's row. `slot_of`: every slot is named by some tile of each owning device.
All inputs are finite; a program needn't handle non-finite values.
Results may differ from the reference program's by a relative error of at most 0.009.
Values may be sent and summed in bfloat16 or wider, within the bound.
A program may use at most 64 MiB of HBM per device.

```python
import jax
import jax.numpy as jnp
from jax import lax

PB = 128
OCC = 1024
KNZ = 16
BLK_DEV = 8
BLOCKS = 512
CAP = 1
N_AMP = 64


def draw_send_list(key, part):
    key = jax.random.fold_in(key, 11)
    count = N_AMP * CAP
    base = jnp.arange(count, dtype=jnp.int32) % BLK_DEV
    keys = jax.random.split(key, N_AMP)
    rows = jax.vmap(lambda k: jax.random.permutation(k, base))(keys)
    return rows.reshape(N_AMP, N_AMP, CAP).astype(jnp.int32)


def draw_slot_of(key, part):
    key = jax.random.fold_in(key, 23)
    count = BLK_DEV * KNZ
    base = jnp.arange(count, dtype=jnp.int32) % (N_AMP * CAP)
    keys = jax.random.split(key, N_AMP)
    rows = jax.vmap(lambda k: jax.random.permutation(k, base))(keys)
    return rows.reshape(N_AMP * BLK_DEV, KNZ).astype(jnp.int32)


def level_of(stream_key, extent, cuts, smallest, largest):
    level = 1.0
    for axis_at, parts in cuts:
        heights = jax.random.uniform(jax.random.fold_in(jax.random.fold_in(stream_key, 6), axis_at), (parts,), jnp.float32, smallest / len(cuts), largest / len(cuts))
        level = level * jnp.repeat(jnp.exp(heights), extent[axis_at] // parts).reshape((-1,) + (1,) * (len(extent) - 1 - axis_at))
    return level


def centred(stream_key, shape, scale, reach, cuts=(), kind=jnp.bfloat16):
    level = level_of(stream_key, shape, cuts, -0.22, 0.18) if cuts else 1.0
    drawn = jax.random.normal(stream_key, shape, jnp.float32) * scale * level
    return jnp.minimum(jnp.maximum(drawn, -reach), reach).astype(kind)


def setup_inputs(seed: int = 0) -> dict:
    splits = jax.random.split(jax.random.key(seed), 6)
    return {
        "amps": centred(splits[0], (BLOCKS, OCC, PB), 1.0, 6.0, ((0, 64), (1, 8))),
        "integrals": centred(splits[1], (BLOCKS, KNZ, PB, PB), (PB * KNZ) ** -0.5, 0.125, ((0, 64), (1, 8))),
        "hole_int": centred(splits[2], (OCC, OCC), OCC ** -0.5, 0.1875),
        "send_list": draw_send_list(jax.random.fold_in(splits[5], 71), 0),
        "slot_of": draw_slot_of(jax.random.fold_in(splits[5], 71), 0),
    }


def reference(amps, integrals, hole_int, send_list, slot_of):
    blocks = amps.shape[0]
    cap = send_list.shape[2]
    blk = blocks // N_AMP
    dest_dev = (jnp.arange(blocks, dtype=jnp.int32) // blk)[:, None]
    src_dev = (slot_of // cap).astype(jnp.int32)
    within = (slot_of % cap).astype(jnp.int32)
    source = src_dev * blk + send_list[src_dev, dest_dev, within]
    hole_wide = hole_int.astype(jnp.float32)

    def one_tile(args):
        index, tiles, own = args
        picked = amps[index].astype(jnp.float32)
        ladder = jnp.einsum("koc,kcd->od", picked, tiles.astype(jnp.float32))
        holes = jnp.dot(hole_wide, own.astype(jnp.float32)).astype(jnp.bfloat16)
        return (ladder + holes.astype(jnp.float32)).astype(jnp.bfloat16)

    return lax.map(one_tile, (source, integrals, amps))
```

```python
import functools

import jax
import jax.numpy as jnp
from jax import lax
from jax.experimental import pallas as pl
from jax.experimental.pallas import tpu as pltpu
from jax.sharding import PartitionSpec as P

MESH = pl.DeviceIdType.MESH
NZ = 16
CT = 2


def kernel(n_amp, n_int, amps, integrals, hole_int, row_list, slot_of, out, *scratch):
    nz = NZ
    ny = n_amp // nz
    nx = n_int // 2
    half = nz // 2
    blk = amps.shape[0]
    occ_dev = amps.shape[1]
    n_chunk = blk // CT

    scratch = list(scratch)
    plus = [amps] + scratch[: half - 1]
    minus = [amps] + scratch[half - 1 : 2 * half - 2]
    far = scratch[2 * half - 2]
    plus.append(far)
    minus.append(far)
    bufs = (plus, minus)
    (meta, meta_s, arrived, picked, all_int, all_amps, rows, held,
     zs, zr, ms, mr, ls, ys, yr, xs, xr, own_sem) = scratch[2 * half - 1 :]

    amp = lax.axis_index("amp")
    me = lax.axis_index("int")
    y, z = amp // nz, amp % nz
    x, core = me // 2, me % 2

    def at_z(shift):
        return y * nz + (z + shift + nz) % nz

    def at_y(shift):
        return ((y + shift) % ny) * nz + z

    def at_x(shift, other=0):
        side = 1 - core if other else core
        return ((x + shift + nx) % nx) * 2 + side

    z_dev = ({"amp": at_z(1)}, {"amp": at_z(-1)})
    partners = list(z_dev)
    partners += [{"amp": at_y(j)} for j in range(1, ny)]
    partners += [{"int": at_x(1)}, {"int": at_x(-1)}, {"int": at_x(0, 1)}]

    own = [
        pltpu.make_async_copy(integrals, all_int.at[me], own_sem.at[0]),
        pltpu.make_async_copy(amps, all_amps.at[me], own_sem.at[1]),
        pltpu.make_async_copy(
            hole_int.at[pl.ds(pl.multiple_of(me * occ_dev, occ_dev), occ_dev)], rows, own_sem.at[2]
        ),
        pltpu.make_async_copy(row_list, meta_s.at[0, 0], own_sem.at[3]),
    ]
    for copy in own:
        copy.start()

    barrier = pltpu.get_barrier_semaphore()
    for partner in partners:
        pl.semaphore_signal(barrier, inc=1, device_id=partner, device_id_type=MESH)
    pl.semaphore_wait(barrier, len(partners))

    sent = []

    def z_copy(d, s, c):
        part = pl.ds(c * CT, CT)
        return pltpu.make_async_remote_copy(
            src_ref=bufs[d][s - 1].at[part],
            dst_ref=bufs[d][s].at[part],
            send_sem=zs.at[d, s, c],
            recv_sem=zr.at[d, s, c],
            device_id=z_dev[d],
            device_id_type=MESH,
        )

    def m_copy(d, s):
        return pltpu.make_async_remote_copy(
            src_ref=row_list if s == 1 else meta.at[d, s - 1],
            dst_ref=meta.at[d, s],
            send_sem=ms.at[d, s],
            recv_sem=mr.at[d, s],
            device_id=z_dev[d],
            device_id_type=MESH,
        )

    def z_goes(d, s, c):
        return s < half or (s == half and (c < n_chunk // 2) == (d == 0))

    def m_goes(d, s):
        return s < half or (s == half and d == 0)

    def z_send(d, s, c):
        copy = z_copy(d, s, c)
        copy.start()
        sent.append(copy)

    def m_send(d, s):
        copy = m_copy(d, s)
        copy.start()
        sent.append(copy)

    def x_piece(ref, slot, p):
        n = blk // 2
        view = ref if slot is None else ref.at[slot]
        return view.at[pl.ds((p % 2) * n, n)]

    def x_copy(kind, p, slot, dev, first=False):
        ref, mine = (all_amps, amps) if p < 2 else (all_int, integrals)
        return pltpu.make_async_remote_copy(
            src_ref=x_piece(mine, None, p) if first else x_piece(ref, slot, p),
            dst_ref=x_piece(ref, slot, p),
            send_sem=xs.at[kind, p],
            recv_sem=xr.at[kind, p],
            device_id=dev,
            device_id_type=MESH,
        )

    x_right, x_left, x_sib = {"int": at_x(1)}, {"int": at_x(-1)}, {"int": at_x(0, 1)}

    def x_send(kind, p, slot, dev, first=False):
        copy = x_copy(kind, p, slot, dev, first)
        copy.start()
        sent.append(copy)

    def x_wait(kind, p, slot):
        x_copy(kind, p, slot, x_sib).wait_recv()

    def y_copy(j, k, slot, dev):
        return pltpu.make_async_remote_copy(
            src_ref=picked.at[j - 1, k],
            dst_ref=arrived.at[slot],
            send_sem=ys.at[j - 1, k],
            recv_sem=yr.at[j - 1, k],
            device_id=dev,
            device_id_type=MESH,
        )

    sources = [(0, 0)]
    for s in range(1, half):
        sources += [(0, s), (1, s)]
    sources.append((0, half))

    def z_of(d, s):
        return (z - s + nz) % nz if d == 0 else (z + s) % nz

    def y_phase(k):
        d, s = sources[k]
        buf = bufs[d][s]
        if s == 0:
            own[3].wait()
        else:
            to_smem = pltpu.make_async_copy(meta.at[d, s], meta_s.at[d, s], ls.at[d, s])
            to_smem.start()
            to_smem.wait()
        src_z = z_of(d, s)
        for j in range(1, ny):
            tile = meta_s[d, s, 0, at_y(j)]
            picked[j - 1, k] = buf[tile]
            copy = y_copy(j, k, y * nz + src_z, {"amp": at_y(j)})
            copy.start()
            sent.append(copy)
        tile = meta_s[d, s, 0, amp]
        arrived[y * nz + src_z] = buf[tile]

    for c in range(n_chunk):
        for d in range(2):
            z_send(d, 1, c)
        if c == 0:
            for d in range(2):
                m_send(d, 1)
    for p in range(4):
        x_send(0, p, me, x_right, first=True)
        x_send(1, p, me, x_left, first=True)
    for p in range(4):
        x_send(2, p, me, x_sib, first=True)

    def x_first_hop():
        for p in range(4):
            x_wait(0, p, at_x(-1))
            if p % 2 == 0:
                x_send(3, p, at_x(-1), x_right)
            x_wait(1, p, at_x(1))
            if p % 2 == 1:
                x_send(4, p, at_x(1), x_left)
        for p in range(4):
            x_send(5, p, at_x(-1), x_sib)
            x_send(6, p, at_x(1), x_sib)

    def x_second_hop():
        for p in range(4):
            x_wait(3 + p % 2, p, at_x(2))
            x_send(7, p, at_x(2), x_sib)

    def x_last():
        for p in range(4):
            x_wait(2, p, at_x(0, 1))
            x_wait(5, p, at_x(-1, 1))
            x_wait(6, p, at_x(1, 1))
            x_wait(7, p, at_x(2, 1))

    def hole_part():
        own[1].wait()
        own[2].wait()

        @pl.loop(0, blk)
        def _(b):
            right = all_amps[:, b].reshape(n_int * occ_dev, -1)
            total = jnp.dot(rows[...], right, preferred_element_type=jnp.float32)
            held[b] = total.astype(jnp.bfloat16)

    y_phase(0)
    for s in range(1, half + 1):
        for c in range(n_chunk):
            for d in range(2):
                if z_goes(d, s, c):
                    z_copy(d, s, c).wait_recv()
                    if s < half and z_goes(d, s + 1, c):
                        z_send(d, s + 1, c)
            if c == 0:
                for d in range(2):
                    if m_goes(d, s):
                        m_copy(d, s).wait_recv()
                        if s < half and m_goes(d, s + 1):
                            m_send(d, s + 1)
        for k, (d, t) in enumerate(sources):
            if t == s:
                y_phase(k)
        if s == half // 2:
            x_first_hop()
        if s == half - 2:
            x_second_hop()
        if s == half - 1:
            x_last()
            hole_part()

    own[0].wait()
    for k, (d, s) in enumerate(sources):
        for j in range(1, ny):
            slot = ((y - j + ny) % ny) * nz + z_of(d, s)
            y_copy(j, k, slot, {"amp": at_y(j)}).wait_recv()

    knz = slot_of.shape[1]
    per = knz // n_int

    @pl.loop(0, blk)
    def _(q):
        total = jnp.zeros(out.shape[1:], jnp.float32)
        for i in range(n_int):
            left = jnp.concatenate([arrived[slot_of[q, i * per + n]] for n in range(per)], axis=1)
            right = all_int[i, q].reshape(left.shape[1], -1)
            total += jnp.dot(left, right, preferred_element_type=jnp.float32)
        out[q] = (total + held[q].astype(jnp.float32)).astype(out.dtype)

    for copy in sent:
        copy.wait_send()


def body(amps, integrals, hole_int, send_list, slot_of):
    n_amp, n_int = lax.axis_size("amp"), lax.axis_size("int")
    blk, occ_dev, width = amps.shape
    half = NZ // 2
    ny = n_amp // NZ
    row_list = jnp.pad(send_list.reshape(1, -1), ((0, 0), (0, 128 - n_amp)))
    tiles = pltpu.VMEM((blk, occ_dev, width), amps.dtype)
    dma = pltpu.SemaphoreType.DMA
    n_chunk = blk // CT
    vmem, anywhere, smem = (pl.BlockSpec(memory_space=m) for m in (pltpu.VMEM, pl.ANY, pltpu.SMEM))
    scratch = [tiles] * (2 * half - 1)
    scratch += [
        pltpu.VMEM((2, half + 1, 1, 128), jnp.int32),
        pltpu.SMEM((2, half + 1, 1, 128), jnp.int32),
        pltpu.VMEM((n_amp, occ_dev, width), amps.dtype),
        pltpu.VMEM((ny - 1, NZ, occ_dev, width), amps.dtype),
        pltpu.VMEM((n_int,) + integrals.shape, integrals.dtype),
        pltpu.VMEM((n_int,) + amps.shape, amps.dtype),
        pltpu.VMEM((occ_dev, hole_int.shape[1]), hole_int.dtype),
        pltpu.VMEM(amps.shape, amps.dtype),
        dma((2, half + 1, n_chunk)),
        dma((2, half + 1, n_chunk)),
        dma((2, half + 1)),
        dma((2, half + 1)),
        dma((2, half + 1)),
        dma((ny - 1, NZ)),
        dma((ny - 1, NZ)),
        dma((8, 4)),
        dma((8, 4)),
        dma((4,)),
    ]
    return pl.pallas_call(
        functools.partial(kernel, n_amp, n_int),
        out_shape=jax.ShapeDtypeStruct(amps.shape, amps.dtype),
        in_specs=[vmem, anywhere, anywhere, vmem, smem],
        out_specs=vmem,
        scratch_shapes=scratch,
        compiler_params=pltpu.CompilerParams(
            collective_id=0, has_side_effects=True, vmem_limit_bytes=40 * 1024 * 1024
        ),
    )(amps, integrals, hole_int, row_list, slot_of)


def solution(mesh):
    in_specs = (
        P("amp", "int", None),
        P("amp", "int", None, None),
        P(),
        P("amp", None, None),
        P("amp", None),
    )
    out_specs = P("amp", "int", None)
    return jax.shard_map(body, mesh=mesh, in_specs=in_specs, out_specs=out_specs, check_vma=False)
```

```python
import functools

import jax
import jax.numpy as jnp
from jax import lax
from jax.experimental import pallas as pl
from jax.experimental.pallas import tpu as pltpu
from jax.sharding import PartitionSpec as P

MESH = pl.DeviceIdType.MESH
NZ = 16
CT = 2


def kernel(n_amp, n_int, amps, integrals, hole_int, row_list, slot_list, out, *scratch):
    nz = NZ
    ny = n_amp // nz
    nx = n_int // 2
    half = nz // 2
    blk = amps.shape[0]
    occ_dev = amps.shape[1]
    n_chunk = blk // CT

    scratch = list(scratch)
    reach = half - 2
    plus = [amps] + scratch[:reach]
    minus = [amps] + scratch[reach : 2 * reach]
    bufs = (plus, minus)
    (mine, meta, meta_s, slot_of, arrived, picked, all_int, all_amps, rows, held, result,
     zs, zr, ms, mr, ls, ys, yr, xs, xr, own_sem, out_sem) = scratch[2 * reach :]

    amp = lax.axis_index("amp")
    me = lax.axis_index("int")
    y, z = amp // nz, amp % nz
    x, core = me // 2, me % 2

    def at_z(shift):
        return y * nz + (z + shift + nz) % nz

    def at_y(shift):
        return ((y + shift) % ny) * nz + z

    def at_x(shift, other=0):
        side = 1 - core if other else core
        return ((x + shift + nx) % nx) * 2 + side

    z_dev = ({"amp": at_z(1)}, {"amp": at_z(-1)})
    partners = list(z_dev)
    partners += [{"amp": at_y(j)} for j in range(1, ny)]
    partners += [{"int": at_x(1)}, {"int": at_x(-1)}, {"int": at_x(0, 1)}]

    own = [
        pltpu.make_async_copy(integrals, all_int.at[me], own_sem.at[0]),
        pltpu.make_async_copy(amps, all_amps.at[me], own_sem.at[1]),
        pltpu.make_async_copy(
            hole_int.at[pl.ds(pl.multiple_of(me * occ_dev, occ_dev), occ_dev)], rows, own_sem.at[2]
        ),
        pltpu.make_async_copy(row_list, meta_s.at[0, 0], own_sem.at[3]),
        pltpu.make_async_copy(slot_list, slot_of, own_sem.at[4]),
        pltpu.make_async_copy(amps, mine, own_sem.at[5]),
    ]
    for copy in own:
        copy.start()

    barrier = pltpu.get_barrier_semaphore()
    for partner in partners:
        pl.semaphore_signal(barrier, inc=1, device_id=partner, device_id_type=MESH)
    pl.semaphore_wait(barrier, len(partners))

    sent = []

    def z_copy(d, s, c):
        part = pl.ds(c * CT, CT)
        return pltpu.make_async_remote_copy(
            src_ref=bufs[d][s - 1].at[part],
            dst_ref=bufs[d][s].at[part],
            send_sem=zs.at[d, s, c],
            recv_sem=zr.at[d, s, c],
            device_id=z_dev[d],
            device_id_type=MESH,
        )

    def m_copy(d, s):
        return pltpu.make_async_remote_copy(
            src_ref=row_list if s == 1 else meta.at[d, s - 1],
            dst_ref=meta.at[d, s],
            send_sem=ms.at[d, s],
            recv_sem=mr.at[d, s],
            device_id=z_dev[d],
            device_id_type=MESH,
        )

    def z_send(d, s, c):
        copy = z_copy(d, s, c)
        copy.start()
        sent.append(copy)

    def m_send(d, s):
        copy = m_copy(d, s)
        copy.start()
        sent.append(copy)

    def x_piece(ref, slot, p):
        n = blk // 2
        view = ref if slot is None else ref.at[slot]
        return view.at[pl.ds((p % 2) * n, n)]

    def x_copy(kind, p, slot, dev, first=False):
        ref, mine = (all_amps, amps) if p < 2 else (all_int, integrals)
        return pltpu.make_async_remote_copy(
            src_ref=x_piece(mine, None, p) if first else x_piece(ref, slot, p),
            dst_ref=x_piece(ref, slot, p),
            send_sem=xs.at[kind, p],
            recv_sem=xr.at[kind, p],
            device_id=dev,
            device_id_type=MESH,
        )

    x_right, x_left, x_sib = {"int": at_x(1)}, {"int": at_x(-1)}, {"int": at_x(0, 1)}

    def x_send(kind, p, slot, dev, first=False):
        copy = x_copy(kind, p, slot, dev, first)
        copy.start()
        sent.append(copy)

    def x_wait(kind, p, slot):
        x_copy(kind, p, slot, x_sib).wait_recv()

    named = []
    near = {}
    for d, t in [(0, 0)] + [(d, t) for t in range(1, reach + 1) for d in range(2)]:
        near[d, t] = range(len(named), len(named) + ny - 1)
        named += [(d, t, j, 0) for j in range(1, ny)]
    beyond = []
    for n in range(ny // 2):
        for d in range(2):
            beyond.append(len(named))
            named.append((d, reach, n + d * (ny // 2), 2 - 4 * d))
    for j in (ny // 2, *range(1, ny // 2), *range(ny // 2 + 1, ny), 0):
        for d in range(2):
            beyond.append(len(named))
            named.append((d, reach, j, 1 - 2 * d))

    def z_of(d, t, shift):
        return (z + shift + (t if d else -t) + nz) % nz

    def n_copy(n, dev, slot):
        return pltpu.make_async_remote_copy(
            src_ref=picked.at[n],
            dst_ref=arrived.at[slot],
            send_sem=ys.at[n],
            recv_sem=yr.at[n],
            device_id=dev,
            device_id_type=MESH,
        )

    def tile_for(d, t, target):
        buf = bufs[d][t] if t else mine
        return buf[meta_s[d, t, 0, target]]

    def n_send(n):
        d, t, j, shift = named[n]
        target = ((y + j) % ny) * nz + (z + shift + nz) % nz
        picked[n] = tile_for(d, t, target)
        copy = n_copy(n, {"amp": target}, y * nz + z_of(d, t, 0))
        copy.start()
        sent.append(copy)

    def n_wait(n):
        d, t, j, shift = named[n]
        slot = ((y - j + ny) % ny) * nz + z_of(d, t, -shift)
        n_copy(n, {"amp": at_y(1)}, slot).wait_recv()

    def to_smem(d, t):
        return pltpu.make_async_copy(meta.at[d, t], meta_s.at[d, t], ls.at[d, t])

    def keep_own(d, t):
        arrived[y * nz + z_of(d, t, 0)] = tile_for(d, t, amp)

    def name_part(t, part):
        for d in range(2):
            if part == 0:
                to_smem(d, t).wait()
            if part < ny - 1:
                n_send(near[d, t][part])
            else:
                keep_own(d, t)

    for c in range(n_chunk):
        for d in range(2):
            z_send(d, 1, c)
        if c == 0:
            for d in range(2):
                m_send(d, 1)
    for p, r in ((2, 3), (0, 1), (3, 2), (1, 0)):
        x_send(0, p, me, x_right, first=True)
        x_send(1, r, me, x_left, first=True)
    for p in range(4):
        x_send(2, p, me, x_sib, first=True)

    def x_stage(stage):
        if stage == 0:
            for p in (2, 0):
                x_wait(0, p, at_x(-1))
                x_send(3, p, at_x(-1), x_right)
                x_wait(1, p + 1, at_x(1))
                x_send(4, p + 1, at_x(1), x_left)
        elif stage == 1:
            for p in (3, 1):
                x_wait(0, p, at_x(-1))
                x_wait(1, p - 1, at_x(1))
            for p in range(4):
                x_send(5, p, at_x(-1), x_sib)
                x_send(6, p, at_x(1), x_sib)
        elif stage == 2:
            for p in range(4):
                x_wait(3 + p % 2, p, at_x(2))
                x_send(7, p, at_x(2), x_sib)
        else:
            for p in range(4):
                x_wait(2, p, at_x(0, 1))
                x_wait(5, p, at_x(-1, 1))
                x_wait(6, p, at_x(1, 1))
                x_wait(7, p, at_x(2, 1))

    def hole_part():
        own[1].wait()
        own[2].wait()

        @pl.loop(0, blk)
        def _(b):
            right = all_amps[:, b].reshape(n_int * occ_dev, -1)
            total = jnp.dot(rows[...], right, preferred_element_type=jnp.float32)
            held[b] = total.astype(jnp.bfloat16)

    own[3].wait()
    own[5].wait()
    for n in near[0, 0]:
        n_send(n)
    keep_own(0, 0)
    for t in range(1, reach + 1):
        for c in range(n_chunk):
            for d in range(2):
                z_copy(d, t, c).wait_recv()
                if t < reach:
                    z_send(d, t + 1, c)
            if c == 0:
                for d in range(2):
                    m_copy(d, t).wait_recv()
                    if t < reach:
                        m_send(d, t + 1)
                    to_smem(d, t).start()
            if t > 1:
                name_part(t - 1, c)
        if t >= reach - 3 and t < reach:
            x_stage(t - reach + 3)
    for d in range(2):
        to_smem(d, reach).wait()
    for n in beyond:
        n_send(n)
    for i in range(ny - 1):
        for d in range(2):
            n_send(near[d, reach][i])
    for d in range(2):
        keep_own(d, reach)
    x_stage(3)
    hole_part()

    own[0].wait()
    own[4].wait()
    for n in range(len(named)):
        n_wait(n)

    knz = slot_of.shape[1]
    per = knz // n_int

    def finish(q):
        return pltpu.make_async_copy(result.at[q], out.at[q], out_sem.at[q])

    for q in range(blk):
        total = jnp.zeros(out.shape[1:], jnp.float32)
        for i in range(n_int):
            left = jnp.concatenate([arrived[slot_of[q, i * per + n]] for n in range(per)], axis=1)
            right = all_int[i, q].reshape(left.shape[1], -1)
            total += jnp.dot(left, right, preferred_element_type=jnp.float32)
        result[q] = (total + held[q].astype(jnp.float32)).astype(out.dtype)
        finish(q).start()

    for copy in sent:
        copy.wait_send()
    for q in range(blk):
        finish(q).wait()


def body(amps, integrals, hole_int, send_list, slot_of):
    n_amp, n_int = lax.axis_size("amp"), lax.axis_size("int")
    blk, occ_dev, width = amps.shape
    half = NZ // 2
    ny = n_amp // NZ
    row_list = send_list.reshape(1, n_amp)
    tiles = pltpu.VMEM((blk, occ_dev, width), amps.dtype)
    dma = pltpu.SemaphoreType.DMA
    n_chunk = blk // CT
    hbm = pl.BlockSpec(memory_space=pltpu.HBM)
    reach = half - 2
    n_named = (2 * reach + 1) * (ny - 1) + 3 * ny
    scratch = [tiles] * (2 * reach)
    scratch += [
        tiles,
        pltpu.VMEM((2, reach + 1, 1, n_amp), jnp.int32),
        pltpu.SMEM((2, reach + 1, 1, n_amp), jnp.int32),
        pltpu.SMEM(slot_of.shape, jnp.int32),
        pltpu.VMEM((n_amp, occ_dev, width), amps.dtype),
        pltpu.VMEM((n_named, occ_dev, width), amps.dtype),
        pltpu.VMEM((n_int,) + integrals.shape, integrals.dtype),
        pltpu.VMEM((n_int,) + amps.shape, amps.dtype),
        pltpu.VMEM((occ_dev, hole_int.shape[1]), hole_int.dtype),
        tiles,
        tiles,
        dma((2, reach + 1, n_chunk)),
        dma((2, reach + 1, n_chunk)),
        dma((2, reach + 1)),
        dma((2, reach + 1)),
        dma((2, reach + 1)),
        dma((n_named,)),
        dma((n_named,)),
        dma((8, 4)),
        dma((8, 4)),
        dma((6,)),
        dma((blk,)),
    ]
    return pl.pallas_call(
        functools.partial(kernel, n_amp, n_int),
        out_shape=jax.ShapeDtypeStruct(amps.shape, amps.dtype),
        in_specs=[hbm] * 5,
        out_specs=hbm,
        scratch_shapes=scratch,
        compiler_params=pltpu.CompilerParams(
            collective_id=0, has_side_effects=True, vmem_limit_bytes=56 * 1024 * 1024
        ),
    )(amps, integrals, hole_int, row_list, slot_of)


def solution(mesh):
    in_specs = (
        P("amp", "int", None),
        P("amp", "int", None, None),
        P(),
        P("amp", None, None),
        P("amp", None),
    )
    out_specs = P("amp", "int", None)
    return jax.shard_map(body, mesh=mesh, in_specs=in_specs, out_specs=out_specs, check_vma=False)
```

```python
import functools

import jax
import jax.numpy as jnp
from jax import lax
from jax.experimental import pallas as pl
from jax.experimental.pallas import tpu as pltpu
from jax.sharding import PartitionSpec as P

MESH = pl.DeviceIdType.MESH
NZ = 16
CT = 2
STAGE = ((0, 1, 0, 1), (1, 0, 1, 0), (3,) * 4, (2,) * 4, (2,) * 4, (3,) * 4, (3,) * 4, (3,) * 4)


def kernel(n_amp, n_int, amps, integrals, hole_int, row_list, slot_list, out, *scratch):
    nz = NZ
    ny = n_amp // nz
    nx = n_int // 2
    half = nz // 2
    blk = amps.shape[0]
    occ_dev = amps.shape[1]
    n_chunk = blk // CT

    scratch = list(scratch)
    reach = half - 2
    plus = [amps] + scratch[:reach]
    minus = [amps] + scratch[reach : 2 * reach]
    bufs = (plus, minus)
    (mine, meta, meta_s, slot_of, arrived, picked, all_int, all_amps, rows, held, result,
     zs, zr, ms, mr, ls, ys, yr, xs, xr, own_sem, out_sem) = scratch[2 * reach :]

    amp = lax.axis_index("amp")
    me = lax.axis_index("int")
    y, z = amp // nz, amp % nz
    x, core = me // 2, me % 2

    def at_z(shift):
        return y * nz + (z + shift + nz) % nz

    def at_y(shift):
        return ((y + shift) % ny) * nz + z

    def at_x(shift, other=0):
        side = 1 - core if other else core
        return ((x + shift + nx) % nx) * 2 + side

    z_dev = ({"amp": at_z(1)}, {"amp": at_z(-1)})
    partners = list(z_dev)
    partners += [{"amp": at_y(j)} for j in range(1, ny)]
    partners += [{"int": at_x(1)}, {"int": at_x(-1)}, {"int": at_x(0, 1)}]

    own = [
        pltpu.make_async_copy(integrals, all_int.at[me], own_sem.at[0]),
        pltpu.make_async_copy(amps, all_amps.at[me], own_sem.at[1]),
        pltpu.make_async_copy(
            hole_int.at[pl.ds(pl.multiple_of(me * occ_dev, occ_dev), occ_dev)], rows, own_sem.at[2]
        ),
        pltpu.make_async_copy(row_list, meta_s.at[0, 0], own_sem.at[3]),
        pltpu.make_async_copy(slot_list, slot_of, own_sem.at[4]),
        pltpu.make_async_copy(amps, mine, own_sem.at[5]),
    ]
    for copy in own:
        copy.start()

    barrier = pltpu.get_barrier_semaphore()
    for partner in partners:
        pl.semaphore_signal(barrier, inc=1, device_id=partner, device_id_type=MESH)
    pl.semaphore_wait(barrier, len(partners))

    def arrival(ref, sem):
        pltpu.make_async_copy(ref, ref, sem).wait()

    def z_copy(d, s, c):
        part = pl.ds(c * CT, CT)
        return pltpu.make_async_remote_copy(
            src_ref=bufs[d][s - 1].at[part],
            dst_ref=bufs[d][s].at[part],
            send_sem=zs,
            recv_sem=zr.at[d, s - 1, c],
            device_id=z_dev[d],
            device_id_type=MESH,
        )

    def m_copy(d, s):
        return pltpu.make_async_remote_copy(
            src_ref=row_list if s == 1 else meta.at[d, s - 1],
            dst_ref=meta.at[d, s],
            send_sem=ms,
            recv_sem=mr.at[d, s - 1],
            device_id=z_dev[d],
            device_id_type=MESH,
        )

    def z_send(d, s, c):
        copy = z_copy(d, s, c)
        copy.start()

    def m_send(d, s):
        copy = m_copy(d, s)
        copy.start()

    def x_piece(ref, slot, p):
        n = blk // 2
        view = ref if slot is None else ref.at[slot]
        return view.at[pl.ds((p % 2) * n, n)]

    def x_copy(kind, p, slot, dev, first=False):
        ref, mine = (all_amps, amps) if p < 2 else (all_int, integrals)
        return pltpu.make_async_remote_copy(
            src_ref=x_piece(mine, None, p) if first else x_piece(ref, slot, p),
            dst_ref=x_piece(ref, slot, p),
            send_sem=xs.at[p // 2],
            recv_sem=xr.at[STAGE[kind][p], p // 2],
            device_id=dev,
            device_id_type=MESH,
        )

    x_right, x_left, x_sib = {"int": at_x(1)}, {"int": at_x(-1)}, {"int": at_x(0, 1)}

    def x_send(kind, p, slot, dev, first=False):
        copy = x_copy(kind, p, slot, dev, first)
        copy.start()

    def x_wait(stage, n):
        for sem, ref in ((0, all_amps), (1, all_int)):
            arrival(ref.at[pl.ds(0, n)], xr.at[stage, sem])

    named = []
    near = {}
    for d, t in [(0, 0)] + [(d, t) for t in range(1, reach + 1) for d in range(2)]:
        near[d, t] = range(len(named), len(named) + ny - 1)
        named += [(d, t, j, 0) for j in range(1, ny)]
    beyond = []
    for n in range(ny // 2):
        for d in range(2):
            beyond.append(len(named))
            named.append((d, reach, n + d * (ny // 2), 2 - 4 * d))
    for j in (ny // 2, *range(1, ny // 2), *range(ny // 2 + 1, ny), 0):
        for d in range(2):
            beyond.append(len(named))
            named.append((d, reach, j, 1 - 2 * d))

    def z_of(d, t, shift):
        return (z + shift + (t if d else -t) + nz) % nz

    def n_copy(n, dev, slot):
        return pltpu.make_async_remote_copy(
            src_ref=picked.at[n],
            dst_ref=arrived.at[slot],
            send_sem=ys,
            recv_sem=yr,
            device_id=dev,
            device_id_type=MESH,
        )

    def tile_for(d, t, target):
        buf = bufs[d][t] if t else mine
        return buf[meta_s[d, t, 0, target]]

    def n_send(n):
        d, t, j, shift = named[n]
        target = ((y + j) % ny) * nz + (z + shift + nz) % nz
        picked[n] = tile_for(d, t, target)
        copy = n_copy(n, {"amp": target}, y * nz + z_of(d, t, 0))
        copy.start()

    def to_smem(d, t):
        return pltpu.make_async_copy(meta.at[d, t], meta_s.at[d, t], ls.at[d])

    def keep_own(d, t):
        arrived[y * nz + z_of(d, t, 0)] = tile_for(d, t, amp)

    def name_part(t, part):
        for d in range(2):
            if part < ny - 1:
                n_send(near[d, t][part])
            else:
                keep_own(d, t)

    for c in range(n_chunk):
        for d in range(2):
            z_send(d, 1, c)
        if c == 0:
            for d in range(2):
                m_send(d, 1)
    for p, r in ((2, 3), (0, 1), (3, 2), (1, 0)):
        x_send(0, p, me, x_right, first=True)
        x_send(1, r, me, x_left, first=True)
    for p in range(4):
        x_send(2, p, me, x_sib, first=True)

    def x_stage(stage):
        if stage == 0:
            x_wait(0, 1)
            for p in (2, 0):
                x_send(3, p, at_x(-1), x_right)
                x_send(4, p + 1, at_x(1), x_left)
        elif stage == 1:
            x_wait(1, 1)
            for p in range(4):
                x_send(5, p, at_x(-1), x_sib)
                x_send(6, p, at_x(1), x_sib)
        elif stage == 2:
            x_wait(2, 1)
            for p in range(4):
                x_send(7, p, at_x(2), x_sib)
        else:
            x_wait(3, n_int // 2)

    def hole_part():
        own[1].wait()
        own[2].wait()

        @pl.loop(0, blk)
        def _(b):
            right = all_amps[:, b].reshape(n_int * occ_dev, -1)
            total = jnp.dot(rows[...], right, preferred_element_type=jnp.float32)
            held[b] = total.astype(jnp.bfloat16)

    own[3].wait()
    own[5].wait()
    for n in near[0, 0]:
        n_send(n)
    keep_own(0, 0)
    for t in range(1, reach + 1):
        for c in range(n_chunk):
            for d in range(2):
                z_copy(d, t, c).wait_recv()
                if t < reach:
                    z_send(d, t + 1, c)
            if c == 0:
                for d in range(2):
                    m_copy(d, t).wait_recv()
                    if t < reach:
                        m_send(d, t + 1)
                    if t > 1:
                        to_smem(d, t - 1).wait()
                    to_smem(d, t).start()
            if t > 1:
                name_part(t - 1, c)
        if t >= reach - 3 and t < reach:
            x_stage(t - reach + 3)
    for d in range(2):
        to_smem(d, reach).wait()
    for n in beyond:
        n_send(n)
    for i in range(ny - 1):
        for d in range(2):
            n_send(near[d, reach][i])
    for d in range(2):
        keep_own(d, reach)
    x_stage(3)
    hole_part()

    own[0].wait()
    own[4].wait()
    arrival(picked, yr)

    knz = slot_of.shape[1]
    per = knz // n_int

    def finish(q):
        return pltpu.make_async_copy(result.at[q], out.at[q], out_sem)

    for q in range(blk):
        total = jnp.zeros(out.shape[1:], jnp.float32)
        for i in range(n_int):
            left = jnp.concatenate([arrived[slot_of[q, i * per + n]] for n in range(per)], axis=1)
            right = all_int[i, q].reshape(left.shape[1], -1)
            total += jnp.dot(left, right, preferred_element_type=jnp.float32)
        result[q] = (total + held[q].astype(jnp.float32)).astype(out.dtype)
        finish(q).start()

    for d in range(2):
        for t in range(1, reach + 1):
            arrival(bufs[d][t], zs)
    arrival(meta.at[:, pl.ds(1, reach)], ms)
    arrival(picked, ys)
    for sem, ref in ((0, all_amps), (1, all_int)):
        arrival(ref.at[pl.ds(0, n_int - 1)], xs.at[sem])
    arrival(out, out_sem)


def body(amps, integrals, hole_int, send_list, slot_of):
    n_amp, n_int = lax.axis_size("amp"), lax.axis_size("int")
    blk, occ_dev, width = amps.shape
    half = NZ // 2
    ny = n_amp // NZ
    row_list = send_list.reshape(1, n_amp)
    tiles = pltpu.VMEM((blk, occ_dev, width), amps.dtype)
    dma = pltpu.SemaphoreType.DMA
    n_chunk = blk // CT
    hbm = pl.BlockSpec(memory_space=pltpu.HBM)
    reach = half - 2
    n_named = (2 * reach + 1) * (ny - 1) + 3 * ny
    scratch = [tiles] * (2 * reach)
    scratch += [
        tiles,
        pltpu.VMEM((2, reach + 1, 1, n_amp), jnp.int32),
        pltpu.SMEM((2, reach + 1, 1, n_amp), jnp.int32),
        pltpu.SMEM(slot_of.shape, jnp.int32),
        pltpu.VMEM((n_amp, occ_dev, width), amps.dtype),
        pltpu.VMEM((n_named, occ_dev, width), amps.dtype),
        pltpu.VMEM((n_int,) + integrals.shape, integrals.dtype),
        pltpu.VMEM((n_int,) + amps.shape, amps.dtype),
        pltpu.VMEM((occ_dev, hole_int.shape[1]), hole_int.dtype),
        tiles,
        tiles,
        dma,
        dma((2, reach, n_chunk)),
        dma,
        dma((2, reach)),
        dma((2,)),
        dma,
        dma,
        dma((2,)),
        dma((4, 2)),
        dma((6,)),
        dma,
    ]
    return pl.pallas_call(
        functools.partial(kernel, n_amp, n_int),
        out_shape=jax.ShapeDtypeStruct(amps.shape, amps.dtype),
        in_specs=[hbm] * 5,
        out_specs=hbm,
        scratch_shapes=scratch,
        compiler_params=pltpu.CompilerParams(
            collective_id=0, has_side_effects=True, vmem_limit_bytes=56 * 1024 * 1024
        ),
    )(amps, integrals, hole_int, row_list, slot_of)


def solution(mesh):
    in_specs = (
        P("amp", "int", None),
        P("amp", "int", None, None),
        P(),
        P("amp", None, None),
        P("amp", None),
    )
    out_specs = P("amp", "int", None)
    return jax.shard_map(body, mesh=mesh, in_specs=in_specs, out_specs=out_specs, check_vma=False)
```

```python
import functools

import jax
import jax.numpy as jnp
from jax import lax
from jax.experimental import pallas as pl
from jax.experimental.pallas import tpu as pltpu
from jax.sharding import PartitionSpec as P

MESH = pl.DeviceIdType.MESH
NZ = 16
REACH = 5
CT = 2
STAGE = ((0, 1, 0, 1), (1, 0, 1, 0), (3,) * 4, (2,) * 4, (2,) * 4, (3,) * 4, (3,) * 4, (3,) * 4)


def kernel(n_amp, n_int, amps, integrals, hole_int, row_list, slot_list, out, *scratch):
    nz = NZ
    ny = n_amp // nz
    nx = n_int // 2
    half = nz // 2
    blk = amps.shape[0]
    occ_dev = amps.shape[1]
    n_chunk = blk // CT

    scratch = list(scratch)
    reach = REACH
    plus = [amps] + scratch[:reach]
    minus = [amps] + scratch[reach : 2 * reach]
    bufs = (plus, minus)
    (mine, meta, meta_s, slot_of, arrived, picked, all_int, all_amps, rows, held,
     zs, zr, ms, mr, ls, ys, yr, xs, xr, own_sem) = scratch[2 * reach :]

    amp = lax.axis_index("amp")
    me = lax.axis_index("int")
    y, z = amp // nz, amp % nz
    x, core = me // 2, me % 2

    def at_z(shift):
        return y * nz + (z + shift + nz) % nz

    def at_y(shift):
        return ((y + shift) % ny) * nz + z

    def at_x(shift, other=0):
        side = 1 - core if other else core
        return ((x + shift + nx) % nx) * 2 + side

    z_dev = ({"amp": at_z(1)}, {"amp": at_z(-1)})
    partners = list(z_dev)
    partners += [{"amp": at_y(j)} for j in range(1, ny)]
    partners += [{"int": at_x(1)}, {"int": at_x(-1)}, {"int": at_x(0, 1)}]

    own = [
        pltpu.make_async_copy(integrals, all_int.at[me], own_sem.at[0]),
        pltpu.make_async_copy(amps, all_amps.at[me], own_sem.at[1]),
        pltpu.make_async_copy(
            hole_int.at[pl.ds(pl.multiple_of(me * occ_dev, occ_dev), occ_dev)], rows, own_sem.at[2]
        ),
        pltpu.make_async_copy(row_list, meta_s.at[0, 0], own_sem.at[3]),
        pltpu.make_async_copy(slot_list, slot_of, own_sem.at[4]),
        pltpu.make_async_copy(amps, mine, own_sem.at[5]),
    ]
    for copy in own:
        copy.start()

    barrier = pltpu.get_barrier_semaphore()
    for partner in partners:
        pl.semaphore_signal(barrier, inc=1, device_id=partner, device_id_type=MESH)
    pl.semaphore_wait(barrier, len(partners))

    def arrival(ref, sem):
        pltpu.make_async_copy(ref, ref, sem).wait()

    def z_copy(d, s, c):
        part = pl.ds(c * CT, CT)
        return pltpu.make_async_remote_copy(
            src_ref=bufs[d][s - 1].at[part],
            dst_ref=bufs[d][s].at[part],
            send_sem=zs,
            recv_sem=zr.at[d, s - 1, c],
            device_id=z_dev[d],
            device_id_type=MESH,
        )

    def m_copy(d, s):
        return pltpu.make_async_remote_copy(
            src_ref=row_list if s == 1 else meta.at[d, s - 1],
            dst_ref=meta.at[d, s],
            send_sem=ms,
            recv_sem=mr.at[d, s - 1],
            device_id=z_dev[d],
            device_id_type=MESH,
        )

    def z_send(d, s, c):
        copy = z_copy(d, s, c)
        copy.start()

    def m_send(d, s):
        copy = m_copy(d, s)
        copy.start()

    def x_piece(ref, slot, p):
        n = blk // 2
        view = ref if slot is None else ref.at[slot]
        return view.at[pl.ds((p % 2) * n, n)]

    def x_copy(kind, p, slot, dev, first=False):
        ref, mine = (all_amps, amps) if p < 2 else (all_int, integrals)
        return pltpu.make_async_remote_copy(
            src_ref=x_piece(mine, None, p) if first else x_piece(ref, slot, p),
            dst_ref=x_piece(ref, slot, p),
            send_sem=xs.at[p // 2],
            recv_sem=xr.at[STAGE[kind][p], p // 2],
            device_id=dev,
            device_id_type=MESH,
        )

    x_right, x_left, x_sib = {"int": at_x(1)}, {"int": at_x(-1)}, {"int": at_x(0, 1)}

    def x_send(kind, p, slot, dev, first=False):
        copy = x_copy(kind, p, slot, dev, first)
        copy.start()

    def x_wait(stage, n):
        for sem, ref in ((0, all_amps), (1, all_int)):
            arrival(ref.at[pl.ds(0, n)], xr.at[stage, sem])

    named = []
    near = {}
    for d, t in [(0, 0)] + [(d, t) for t in range(1, reach + 1) for d in range(2)]:
        near[d, t] = range(len(named), len(named) + ny - 1)
        named += [(d, t, j, 0) for j in range(1, ny)]
    beyond = {}
    for h in range(1, half - reach + 1):
        for j in range(ny):
            for d in range(2):
                if reach + h < half or j // (ny // 2) == d:
                    beyond[h, j, d] = len(named)
                    named.append((d, reach, j, h - 2 * d * h))

    def z_of(d, t, shift):
        return (z + shift + (t if d else -t) + nz) % nz

    def n_copy(n, dev, slot):
        return pltpu.make_async_remote_copy(
            src_ref=picked.at[n],
            dst_ref=arrived.at[slot],
            send_sem=ys,
            recv_sem=yr,
            device_id=dev,
            device_id_type=MESH,
        )

    def tile_for(d, t, target):
        buf = bufs[d][t] if t else mine
        return buf[meta_s[d, t, 0, target]]

    def n_send(n):
        d, t, j, shift = named[n]
        target = ((y + j) % ny) * nz + (z + shift + nz) % nz
        picked[n] = tile_for(d, t, target)
        copy = n_copy(n, {"amp": target}, y * nz + z_of(d, t, 0))
        copy.start()

    def to_smem(d, t):
        return pltpu.make_async_copy(meta.at[d, t], meta_s.at[d, t], ls.at[d])

    def keep_own(d, t):
        arrived[y * nz + z_of(d, t, 0)] = tile_for(d, t, amp)

    def name_part(t, part):
        for d in range(2):
            if part < ny - 1:
                n_send(near[d, t][part])
            else:
                keep_own(d, t)

    for c in range(n_chunk):
        for d in range(2):
            z_send(d, 1, c)
        if c == 0:
            for d in range(2):
                m_send(d, 1)
    for p, r in ((2, 3), (0, 1), (3, 2), (1, 0)):
        x_send(0, p, me, x_right, first=True)
        x_send(1, r, me, x_left, first=True)
    for p in range(4):
        x_send(2, p, me, x_sib, first=True)

    def x_stage(stage):
        if stage == 0:
            x_wait(0, 1)
            for p in (2, 0):
                x_send(3, p, at_x(-1), x_right)
                x_send(4, p + 1, at_x(1), x_left)
        elif stage == 1:
            x_wait(1, 1)
            for p in range(4):
                x_send(5, p, at_x(-1), x_sib)
                x_send(6, p, at_x(1), x_sib)
        elif stage == 2:
            x_wait(2, 1)
            for p in range(4):
                x_send(7, p, at_x(2), x_sib)
        else:
            x_wait(3, n_int // 2)

    def hole_part():
        own[1].wait()
        own[2].wait()

        @pl.loop(0, blk)
        def _(b):
            right = all_amps[:, b].reshape(n_int * occ_dev, -1)
            total = jnp.dot(rows[...], right, preferred_element_type=jnp.float32)
            held[b] = total.astype(jnp.bfloat16)

    own[3].wait()
    own[5].wait()
    for n in near[0, 0]:
        n_send(n)
    keep_own(0, 0)
    for t in range(1, reach + 1):
        for c in range(n_chunk):
            for d in range(2):
                z_copy(d, t, c).wait_recv()
                if t < reach:
                    z_send(d, t + 1, c)
            if c == 0:
                for d in range(2):
                    m_copy(d, t).wait_recv()
                    if t < reach:
                        m_send(d, t + 1)
                    if t > 1:
                        to_smem(d, t - 1).wait()
                    to_smem(d, t).start()
            if t > 1:
                name_part(t - 1, c)
        if t >= reach - 3 and t < reach:
            x_stage(t - reach + 3)
    for d in range(2):
        to_smem(d, reach).wait()
    by_y = (2, 1, 3, 0)
    for h in range(half - reach, 0, -1):
        for j in by_y:
            for d in range(2):
                if (h, j, d) in beyond:
                    n_send(beyond[h, j, d])
    for j in by_y[:-1]:
        for d in range(2):
            n_send(near[d, reach][j - 1])
    for d in range(2):
        keep_own(d, reach)
    x_stage(3)
    hole_part()

    own[0].wait()
    own[4].wait()
    arrival(picked, yr)

    knz = slot_of.shape[1]
    per = knz // n_int

    for q in range(blk):
        total = jnp.zeros(out.shape[1:], jnp.float32)
        for i in range(n_int):
            left = jnp.concatenate([arrived[slot_of[q, i * per + n]] for n in range(per)], axis=1)
            right = all_int[i, q].reshape(left.shape[1], -1)
            total += jnp.dot(left, right, preferred_element_type=jnp.float32)
        out[q] = (total + held[q].astype(jnp.float32)).astype(out.dtype)

    for d in range(2):
        for t in range(1, reach + 1):
            arrival(bufs[d][t], zs)
    arrival(meta.at[:, pl.ds(1, reach)], ms)
    arrival(picked, ys)
    for sem, ref in ((0, all_amps), (1, all_int)):
        arrival(ref.at[pl.ds(0, n_int - 1)], xs.at[sem])


def body(amps, integrals, hole_int, send_list, slot_of):
    n_amp, n_int = lax.axis_size("amp"), lax.axis_size("int")
    blk, occ_dev, width = amps.shape
    half = NZ // 2
    ny = n_amp // NZ
    row_list = send_list.reshape(1, n_amp)
    tiles = pltpu.VMEM((blk, occ_dev, width), amps.dtype)
    dma = pltpu.SemaphoreType.DMA
    n_chunk = blk // CT
    hbm = pl.BlockSpec(memory_space=pltpu.HBM)
    operands = (amps, integrals, hole_int, row_list, slot_of)
    reach = REACH
    n_named = (2 * reach + 1) * (ny - 1) + (2 * (half - reach) - 1) * ny
    scratch = [tiles] * (2 * reach)
    scratch += [
        tiles,
        pltpu.VMEM((2, reach + 1, 1, n_amp), jnp.int32),
        pltpu.SMEM((2, reach + 1, 1, n_amp), jnp.int32),
        pltpu.SMEM(slot_of.shape, jnp.int32),
        pltpu.VMEM((n_amp, occ_dev, width), amps.dtype),
        pltpu.VMEM((n_named, occ_dev, width), amps.dtype),
        pltpu.VMEM((n_int,) + integrals.shape, integrals.dtype),
        pltpu.VMEM((n_int,) + amps.shape, amps.dtype),
        pltpu.VMEM((occ_dev, hole_int.shape[1]), hole_int.dtype),
        tiles,
        dma,
        dma((2, reach, n_chunk)),
        dma,
        dma((2, reach)),
        dma((2,)),
        dma,
        dma,
        dma((2,)),
        dma((4, 2)),
        dma((6,)),
    ]
    return pl.pallas_call(
        functools.partial(kernel, n_amp, n_int),
        out_shape=jax.ShapeDtypeStruct(amps.shape, amps.dtype),
        in_specs=[hbm] * len(operands),
        out_specs=pl.BlockSpec(memory_space=pltpu.VMEM),
        scratch_shapes=scratch,
        compiler_params=pltpu.CompilerParams(
            collective_id=0, has_side_effects=True, vmem_limit_bytes=48 * 1024 * 1024
        ),
    )(*(pltpu.with_memory_space_constraint(a, pltpu.HBM) for a in operands))


def solution(mesh):
    in_specs = (
        P("amp", "int", None),
        P("amp", "int", None, None),
        P(),
        P("amp", None, None),
        P("amp", None),
    )
    out_specs = P("amp", "int", None)
    return jax.shard_map(body, mesh=mesh, in_specs=in_specs, out_specs=out_specs, check_vma=False)
```

```python
import functools

import jax
import jax.numpy as jnp
from jax import lax
from jax.experimental import pallas as pl
from jax.experimental.pallas import tpu as pltpu
from jax.sharding import PartitionSpec as P

MESH = pl.DeviceIdType.MESH
NZ = 16
REACH = 5
FIRST = 2
CT = 2
STAGE = ((0, 1, 0, 1), (1, 0, 1, 0), (3,) * 4, (2,) * 4, (2,) * 4, (3,) * 4, (3,) * 4, (3,) * 4)


def kernel(n_amp, n_int, amps, integrals, hole_int, row_list, slot_list, out, *scratch):
    nz = NZ
    ny = n_amp // nz
    nx = n_int // 2
    half = nz // 2
    blk = amps.shape[0]
    occ_dev = amps.shape[1]
    n_chunk = blk // CT

    scratch = list(scratch)
    reach = REACH
    plus = [amps] + scratch[:reach]
    minus = [amps] + scratch[reach : 2 * reach]
    bufs = (plus, minus)
    (mine, meta, meta_s, slot_of, arrived, picked, all_int, all_amps, rows, held,
     zs, zr, ms, mr, ls, ys, yr, xs, xr, own_sem) = scratch[2 * reach :]

    amp = lax.axis_index("amp")
    me = lax.axis_index("int")
    y, z = amp // nz, amp % nz
    x, core = me // 2, me % 2

    def at_z(shift):
        return y * nz + (z + shift + nz) % nz

    def at_y(shift):
        return ((y + shift) % ny) * nz + z

    def at_x(shift, other=0):
        side = 1 - core if other else core
        return ((x + shift + nx) % nx) * 2 + side

    z_dev = ({"amp": at_z(1)}, {"amp": at_z(-1)})
    partners = list(z_dev)
    partners += [{"amp": at_y(j)} for j in range(1, ny)]
    partners += [{"int": at_x(1)}, {"int": at_x(-1)}, {"int": at_x(0, 1)}]

    own = [
        pltpu.make_async_copy(integrals, all_int.at[me], own_sem.at[0]),
        pltpu.make_async_copy(amps, all_amps.at[me], own_sem.at[1]),
        pltpu.make_async_copy(
            hole_int.at[pl.ds(pl.multiple_of(me * occ_dev, occ_dev), occ_dev)], rows, own_sem.at[2]
        ),
        pltpu.make_async_copy(row_list, meta_s.at[0, 0], own_sem.at[3]),
        pltpu.make_async_copy(slot_list, slot_of, own_sem.at[4]),
        pltpu.make_async_copy(amps, mine, own_sem.at[5]),
    ]
    for copy in own:
        copy.start()

    barrier = pltpu.get_barrier_semaphore()
    for partner in partners:
        pl.semaphore_signal(barrier, inc=1, device_id=partner, device_id_type=MESH)
    pl.semaphore_wait(barrier, len(partners))

    def arrival(ref, sem):
        pltpu.make_async_copy(ref, ref, sem).wait()

    def z_copy(d, s, c):
        part = pl.ds(c * CT, CT)
        return pltpu.make_async_remote_copy(
            src_ref=bufs[d][s - 1].at[part],
            dst_ref=bufs[d][s].at[part],
            send_sem=zs,
            recv_sem=zr.at[d, s - 1, c],
            device_id=z_dev[d],
            device_id_type=MESH,
        )

    def m_copy(d, s):
        return pltpu.make_async_remote_copy(
            src_ref=row_list if s == 1 else meta.at[d, s - 1],
            dst_ref=meta.at[d, s],
            send_sem=ms,
            recv_sem=mr.at[d, s - 1],
            device_id=z_dev[d],
            device_id_type=MESH,
        )

    def z_send(d, s, c):
        copy = z_copy(d, s, c)
        copy.start()

    def m_send(d, s):
        copy = m_copy(d, s)
        copy.start()

    def x_piece(ref, slot, p):
        n = blk // 2
        view = ref if slot is None else ref.at[slot]
        return view.at[pl.ds((p % 2) * n, n)]

    def x_copy(kind, p, slot, dev, first=False):
        ref, mine = (all_amps, amps) if p < 2 else (all_int, integrals)
        return pltpu.make_async_remote_copy(
            src_ref=x_piece(mine, None, p) if first else x_piece(ref, slot, p),
            dst_ref=x_piece(ref, slot, p),
            send_sem=xs.at[p // 2],
            recv_sem=xr.at[STAGE[kind][p], p // 2],
            device_id=dev,
            device_id_type=MESH,
        )

    x_right, x_left, x_sib = {"int": at_x(1)}, {"int": at_x(-1)}, {"int": at_x(0, 1)}

    def x_send(kind, p, slot, dev, first=False):
        copy = x_copy(kind, p, slot, dev, first)
        copy.start()

    def x_wait(stage, n):
        for sem, ref in ((0, all_amps), (1, all_int)):
            arrival(ref.at[pl.ds(0, n)], xr.at[stage, sem])

    named = []
    near = {}
    for d, t in [(0, 0)] + [(d, t) for t in range(1, reach + 1) for d in range(2)]:
        near[d, t] = range(len(named), len(named) + ny - 1)
        named += [(d, t, j, 0) for j in range(1, ny)]
    beyond = {}
    for h in range(1, half - reach + 1):
        for j in range(ny):
            for d in range(2):
                if reach + h < half or j // (ny // 2) == d:
                    beyond[h, j, d] = len(named)
                    named.append((d, reach, j, h - 2 * d * h))
    n_even = len(named)
    top = half - reach
    uneven = []
    for j in range(ny // 2):
        uneven.append(len(named))
        named.append((1, reach, j, -top))
    target_first = [(z + shift + nz) % nz < FIRST for shift in (top, -top)]

    def z_of(d, t, shift):
        return (z + shift + (t if d else -t) + nz) % nz

    def n_copy(n, dev, slot):
        return pltpu.make_async_remote_copy(
            src_ref=picked.at[n],
            dst_ref=arrived.at[slot],
            send_sem=ys,
            recv_sem=yr,
            device_id=dev,
            device_id_type=MESH,
        )

    def tile_for(d, t, target):
        buf = bufs[d][t] if t else mine
        return buf[meta_s[d, t, 0, target]]

    def n_send(n):
        d, t, j, shift = named[n]
        target = ((y + j) % ny) * nz + (z + shift + nz) % nz
        picked[n] = tile_for(d, t, target)
        copy = n_copy(n, {"amp": target}, y * nz + z_of(d, t, 0))
        copy.start()

    def to_smem(d, t):
        return pltpu.make_async_copy(meta.at[d, t], meta_s.at[d, t], ls.at[d])

    def keep_own(d, t):
        arrived[y * nz + z_of(d, t, 0)] = tile_for(d, t, amp)

    def name_part(t, part):
        for d in range(2):
            if part < ny - 1:
                n_send(near[d, t][part])
            else:
                keep_own(d, t)

    for c in range(n_chunk):
        for d in range(2):
            z_send(d, 1, c)
        if c == 0:
            for d in range(2):
                m_send(d, 1)
    for p, r in ((2, 3), (0, 1), (3, 2), (1, 0)):
        x_send(0, p, me, x_right, first=True)
        x_send(1, r, me, x_left, first=True)
    for p in range(4):
        x_send(2, p, me, x_sib, first=True)

    def x_stage(stage):
        if stage == 0:
            x_wait(0, 1)
            for p in (2, 0):
                x_send(3, p, at_x(-1), x_right)
                x_send(4, p + 1, at_x(1), x_left)
        elif stage == 1:
            x_wait(1, 1)
            for p in range(4):
                x_send(5, p, at_x(-1), x_sib)
                x_send(6, p, at_x(1), x_sib)
        elif stage == 2:
            x_wait(2, 1)
            for p in range(4):
                x_send(7, p, at_x(2), x_sib)
        else:
            x_wait(3, n_int // 2)

    def hole_part():
        own[1].wait()
        own[2].wait()

        @pl.loop(0, blk)
        def _(b):
            right = all_amps[:, b].reshape(n_int * occ_dev, -1)
            total = jnp.dot(rows[...], right, preferred_element_type=jnp.float32)
            held[b] = total.astype(jnp.bfloat16)

    own[3].wait()
    own[5].wait()
    for n in near[0, 0]:
        n_send(n)
    keep_own(0, 0)
    for t in range(1, reach + 1):
        for c in range(n_chunk):
            for d in range(2):
                z_copy(d, t, c).wait_recv()
                if t < reach:
                    z_send(d, t + 1, c)
            if c == 0:
                for d in range(2):
                    m_copy(d, t).wait_recv()
                    if t < reach:
                        m_send(d, t + 1)
                    if t > 1:
                        to_smem(d, t - 1).wait()
                    to_smem(d, t).start()
            if t > 1:
                name_part(t - 1, c)
        if t >= reach - 3 and t < reach:
            x_stage(t - reach + 3)
    for d in range(2):
        to_smem(d, reach).wait()
    by_y = (2, 1, 3, 0)

    def far_send(d, h):
        for j in by_y:
            if (h, j, d) in beyond:
                n_send(beyond[h, j, d])

    def far_uneven():
        for n in uneven:
            n_send(n)

    pl.when(jnp.logical_not(target_first[0]))(functools.partial(far_send, 0, top))
    far_send(1, top)
    pl.when(target_first[1])(far_uneven)
    for h in range(top - 1, 0, -1):
        for j in by_y:
            for d in range(2):
                n_send(beyond[h, j, d])
    for j in by_y[:-1]:
        for d in range(2):
            n_send(near[d, reach][j - 1])
    for d in range(2):
        keep_own(d, reach)
    x_stage(3)
    hole_part()

    own[0].wait()
    own[4].wait()
    arrival(picked.at[pl.ds(0, n_even)], yr)

    knz = slot_of.shape[1]
    per = knz // n_int

    for q in range(blk):
        total = jnp.zeros(out.shape[1:], jnp.float32)
        for i in range(n_int):
            left = jnp.concatenate([arrived[slot_of[q, i * per + n]] for n in range(per)], axis=1)
            right = all_int[i, q].reshape(left.shape[1], -1)
            total += jnp.dot(left, right, preferred_element_type=jnp.float32)
        out[q] = (total + held[q].astype(jnp.float32)).astype(out.dtype)

    for d in range(2):
        for t in range(1, reach + 1):
            arrival(bufs[d][t], zs)
    arrival(meta.at[:, pl.ds(1, reach)], ms)
    n_split = ny // 2

    def sent_split():
        arrival(picked.at[pl.ds(0, n_split)], ys)

    arrival(picked.at[pl.ds(0, n_even - n_split)], ys)
    pl.when(jnp.logical_not(target_first[0]))(sent_split)
    pl.when(target_first[1])(sent_split)
    for sem, ref in ((0, all_amps), (1, all_int)):
        arrival(ref.at[pl.ds(0, n_int - 1)], xs.at[sem])


def body(amps, integrals, hole_int, send_list, slot_of):
    n_amp, n_int = lax.axis_size("amp"), lax.axis_size("int")
    blk, occ_dev, width = amps.shape
    half = NZ // 2
    ny = n_amp // NZ
    row_list = send_list.reshape(1, n_amp)
    tiles = pltpu.VMEM((blk, occ_dev, width), amps.dtype)
    dma = pltpu.SemaphoreType.DMA
    n_chunk = blk // CT
    hbm = pl.BlockSpec(memory_space=pltpu.HBM)
    operands = (amps, integrals, hole_int, row_list, slot_of)
    reach = REACH
    n_named = (2 * reach + 1) * (ny - 1) + (2 * (half - reach) - 1) * ny + ny // 2
    scratch = [tiles] * (2 * reach)
    scratch += [
        tiles,
        pltpu.VMEM((2, reach + 1, 1, n_amp), jnp.int32),
        pltpu.SMEM((2, reach + 1, 1, n_amp), jnp.int32),
        pltpu.SMEM(slot_of.shape, jnp.int32),
        pltpu.VMEM((n_amp, occ_dev, width), amps.dtype),
        pltpu.VMEM((n_named, occ_dev, width), amps.dtype),
        pltpu.VMEM((n_int,) + integrals.shape, integrals.dtype),
        pltpu.VMEM((n_int,) + amps.shape, amps.dtype),
        pltpu.VMEM((occ_dev, hole_int.shape[1]), hole_int.dtype),
        tiles,
        dma,
        dma((2, reach, n_chunk)),
        dma,
        dma((2, reach)),
        dma((2,)),
        dma,
        dma,
        dma((2,)),
        dma((4, 2)),
        dma((6,)),
    ]
    return pl.pallas_call(
        functools.partial(kernel, n_amp, n_int),
        out_shape=jax.ShapeDtypeStruct(amps.shape, amps.dtype),
        in_specs=[hbm] * len(operands),
        out_specs=pl.BlockSpec(memory_space=pltpu.VMEM),
        scratch_shapes=scratch,
        compiler_params=pltpu.CompilerParams(
            collective_id=0, has_side_effects=True, vmem_limit_bytes=48 * 1024 * 1024
        ),
    )(*(pltpu.with_memory_space_constraint(a, pltpu.HBM) for a in operands))


def solution(mesh):
    in_specs = (
        P("amp", "int", None),
        P("amp", "int", None, None),
        P(),
        P("amp", None, None),
        P("amp", None),
    )
    out_specs = P("amp", "int", None)
    return jax.shard_map(body, mesh=mesh, in_specs=in_specs, out_specs=out_specs, check_vma=False)
```

```python
import functools

import jax
import jax.numpy as jnp
from jax import lax
from jax.experimental import pallas as pl
from jax.experimental.pallas import tpu as pltpu
from jax.sharding import PartitionSpec as P

MESH = pl.DeviceIdType.MESH
NZ = 16
REACH = 5
FIRST = 2
CT = 2
STAGE = ((0, 1, 0, 1), (1, 0, 1, 0), (3,) * 4, (2,) * 4, (2,) * 4, (3,) * 4, (3,) * 4, (3,) * 4)


def kernel(n_amp, n_int, amps, integrals, hole_int, row_list, slot_list, out, *scratch):
    nz = NZ
    ny = n_amp // nz
    nx = n_int // 2
    half = nz // 2
    blk = amps.shape[0]
    occ_dev = amps.shape[1]
    n_chunk = blk // CT

    scratch = list(scratch)
    reach = REACH
    plus = [amps] + scratch[:reach]
    minus = [amps] + scratch[reach : 2 * reach]
    bufs = (plus, minus)
    (mine, meta, meta_s, slot_of, arrived, picked, all_int, all_amps, rows, held,
     zs, zr, ms, mr, ls, ys, yr, xs, xr, own_sem) = scratch[2 * reach :]

    amp = lax.axis_index("amp")
    me = lax.axis_index("int")
    y, z = amp // nz, amp % nz
    x, core = me // 2, me % 2

    def at_z(shift):
        return y * nz + (z + shift + nz) % nz

    def at_y(shift):
        return ((y + shift) % ny) * nz + z

    def at_x(shift, other=0):
        side = 1 - core if other else core
        return ((x + shift + nx) % nx) * 2 + side

    z_dev = ({"amp": at_z(1)}, {"amp": at_z(-1)})
    partners = list(z_dev)
    partners += [{"amp": at_y(j)} for j in range(1, ny)]
    partners += [{"int": at_x(1)}, {"int": at_x(-1)}, {"int": at_x(0, 1)}]

    own = [
        pltpu.make_async_copy(integrals, all_int.at[me], own_sem.at[0]),
        pltpu.make_async_copy(amps, all_amps.at[me], own_sem.at[1]),
        pltpu.make_async_copy(
            hole_int.at[pl.ds(pl.multiple_of(me * occ_dev, occ_dev), occ_dev)], rows, own_sem.at[2]
        ),
        pltpu.make_async_copy(row_list, meta_s.at[0, 0], own_sem.at[3]),
        pltpu.make_async_copy(slot_list, slot_of, own_sem.at[4]),
        pltpu.make_async_copy(amps, mine, own_sem.at[5]),
    ]
    for copy in own:
        copy.start()

    barrier = pltpu.get_barrier_semaphore()
    for partner in partners:
        pl.semaphore_signal(barrier, inc=1, device_id=partner, device_id_type=MESH)
    pl.semaphore_wait(barrier, len(partners))

    def arrival(ref, sem):
        pltpu.make_async_copy(ref, ref, sem).wait()

    def z_copy(d, s, c):
        part = pl.ds(c * CT, CT)
        return pltpu.make_async_remote_copy(
            src_ref=bufs[d][s - 1].at[part],
            dst_ref=bufs[d][s].at[part],
            send_sem=zs,
            recv_sem=zr.at[d, s - 1, c],
            device_id=z_dev[d],
            device_id_type=MESH,
        )

    def m_copy(d, s):
        return pltpu.make_async_remote_copy(
            src_ref=row_list if s == 1 else meta.at[d, s - 1],
            dst_ref=meta.at[d, s],
            send_sem=ms,
            recv_sem=mr.at[d, s - 1],
            device_id=z_dev[d],
            device_id_type=MESH,
        )

    def z_send(d, s, c):
        copy = z_copy(d, s, c)
        copy.start()

    def m_send(d, s):
        copy = m_copy(d, s)
        copy.start()

    def x_piece(ref, slot, p):
        n = blk // 2
        view = ref if slot is None else ref.at[slot]
        return view.at[pl.ds((p % 2) * n, n)]

    def x_copy(kind, p, slot, dev, first=False):
        ref, mine = (all_amps, amps) if p < 2 else (all_int, integrals)
        return pltpu.make_async_remote_copy(
            src_ref=x_piece(mine, None, p) if first else x_piece(ref, slot, p),
            dst_ref=x_piece(ref, slot, p),
            send_sem=xs.at[p // 2],
            recv_sem=xr.at[STAGE[kind][p], p // 2],
            device_id=dev,
            device_id_type=MESH,
        )

    x_right, x_left, x_sib = {"int": at_x(1)}, {"int": at_x(-1)}, {"int": at_x(0, 1)}

    def x_send(kind, p, slot, dev, first=False):
        copy = x_copy(kind, p, slot, dev, first)
        copy.start()

    def x_wait(stage, n):
        for sem, ref in ((0, all_amps), (1, all_int)):
            arrival(ref.at[pl.ds(0, n)], xr.at[stage, sem])

    named = []
    near = {}
    for d, t in [(0, 0)] + [(d, t) for t in range(1, reach + 1) for d in range(2)]:
        near[d, t] = range(len(named), len(named) + ny - 1)
        named += [(d, t, j, 0) for j in range(1, ny)]
    beyond = {}
    for h in range(1, half - reach + 1):
        for j in range(ny):
            for d in range(2):
                if reach + h < half or j // (ny // 2) == d:
                    beyond[h, j, d] = len(named)
                    named.append((d, reach, j, h - 2 * d * h))
    n_even = len(named)
    top = half - reach
    uneven = []
    for j in range(ny // 2):
        uneven.append(len(named))
        named.append((1, reach, j, -top))
    target_first = [(z + shift + nz) % nz < FIRST for shift in (top, -top)]

    def z_of(d, t, shift):
        return (z + shift + (t if d else -t) + nz) % nz

    def n_copy(n, dev, slot):
        return pltpu.make_async_remote_copy(
            src_ref=picked.at[n],
            dst_ref=arrived.at[slot],
            send_sem=ys,
            recv_sem=yr,
            device_id=dev,
            device_id_type=MESH,
        )

    def tile_for(d, t, target):
        buf = bufs[d][t] if t else mine
        return buf[meta_s[d, t, 0, target]]

    def n_send(n):
        d, t, j, shift = named[n]
        target = ((y + j) % ny) * nz + (z + shift + nz) % nz
        picked[n] = tile_for(d, t, target)
        copy = n_copy(n, {"amp": target}, y * nz + z_of(d, t, 0))
        copy.start()

    def to_smem(d, t):
        return pltpu.make_async_copy(meta.at[d, t], meta_s.at[d, t], ls.at[d])

    def keep_own(d, t):
        arrived[y * nz + z_of(d, t, 0)] = tile_for(d, t, amp)

    def name_part(t, part):
        for d in range(2):
            if part < ny - 1:
                n_send(near[d, t][part])
            else:
                keep_own(d, t)

    for c in range(n_chunk):
        for d in range(2):
            z_send(d, 1, c)
        if c == 0:
            for d in range(2):
                m_send(d, 1)
    for p, r in ((2, 3), (0, 1), (3, 2), (1, 0)):
        x_send(0, p, me, x_right, first=True)
        x_send(1, r, me, x_left, first=True)
    for p in range(4):
        x_send(2, p, me, x_sib, first=True)

    def x_stage(stage):
        if stage == 0:
            x_wait(0, 1)
            for p in (2, 0):
                x_send(3, p, at_x(-1), x_right)
                x_send(4, p + 1, at_x(1), x_left)
        elif stage == 1:
            x_wait(1, 1)
            for p in range(4):
                x_send(5, p, at_x(-1), x_sib)
                x_send(6, p, at_x(1), x_sib)
        elif stage == 2:
            x_wait(2, 1)
            for p in range(4):
                x_send(7, p, at_x(2), x_sib)
        else:
            x_wait(3, n_int // 2)

    def hole_part():
        own[1].wait()
        own[2].wait()

        @pl.loop(0, blk)
        def _(b):
            right = all_amps[:, b].reshape(n_int * occ_dev, -1)
            total = jnp.dot(rows[...], right, preferred_element_type=jnp.float32)
            held[b] = total.astype(jnp.bfloat16)

    own[3].wait()
    own[5].wait()
    for n in near[0, 0]:
        n_send(n)
    keep_own(0, 0)
    for t in range(1, reach + 1):
        for c in range(n_chunk):
            for d in range(2):
                z_copy(d, t, c).wait_recv()
                if t < reach:
                    z_send(d, t + 1, c)
            if c == 0:
                for d in range(2):
                    m_copy(d, t).wait_recv()
                    if t < reach:
                        m_send(d, t + 1)
                    if t > 1:
                        to_smem(d, t - 1).wait()
                    to_smem(d, t).start()
            if t > 1:
                name_part(t - 1, c)
        if t == reach - 1:
            x_stage(0)
    for d in range(2):
        to_smem(d, reach).wait()
    by_y = (2, 1, 3, 0)

    def far_send(d, h):
        for j in by_y:
            if (h, j, d) in beyond:
                n_send(beyond[h, j, d])

    def far_uneven():
        for n in uneven:
            n_send(n)

    pl.when(jnp.logical_not(target_first[0]))(functools.partial(far_send, 0, top))
    far_send(1, top)
    pl.when(target_first[1])(far_uneven)
    for h in range(top - 1, 0, -1):
        for j in by_y:
            for d in range(2):
                n_send(beyond[h, j, d])
    for j in by_y[:-1]:
        for d in range(2):
            n_send(near[d, reach][j - 1])
    for d in range(2):
        keep_own(d, reach)
    x_stage(1)
    x_stage(2)
    x_stage(3)
    hole_part()

    own[0].wait()
    own[4].wait()
    arrival(picked.at[pl.ds(0, n_even)], yr)

    knz = slot_of.shape[1]
    per = knz // n_int

    for q in range(blk):
        total = jnp.zeros(out.shape[1:], jnp.float32)
        for i in range(n_int):
            left = jnp.concatenate([arrived[slot_of[q, i * per + n]] for n in range(per)], axis=1)
            right = all_int[i, q].reshape(left.shape[1], -1)
            total += jnp.dot(left, right, preferred_element_type=jnp.float32)
        out[q] = (total + held[q].astype(jnp.float32)).astype(out.dtype)

    for d in range(2):
        for t in range(1, reach + 1):
            arrival(bufs[d][t], zs)
    arrival(meta.at[:, pl.ds(1, reach)], ms)
    n_split = ny // 2

    def sent_split():
        arrival(picked.at[pl.ds(0, n_split)], ys)

    arrival(picked.at[pl.ds(0, n_even - n_split)], ys)
    pl.when(jnp.logical_not(target_first[0]))(sent_split)
    pl.when(target_first[1])(sent_split)
    for sem, ref in ((0, all_amps), (1, all_int)):
        arrival(ref.at[pl.ds(0, n_int - 1)], xs.at[sem])


def body(amps, integrals, hole_int, send_list, slot_of):
    n_amp, n_int = lax.axis_size("amp"), lax.axis_size("int")
    blk, occ_dev, width = amps.shape
    half = NZ // 2
    ny = n_amp // NZ
    row_list = send_list.reshape(1, n_amp)
    tiles = pltpu.VMEM((blk, occ_dev, width), amps.dtype)
    dma = pltpu.SemaphoreType.DMA
    n_chunk = blk // CT
    hbm = pl.BlockSpec(memory_space=pltpu.HBM)
    operands = (amps, integrals, hole_int, row_list, slot_of)
    reach = REACH
    n_named = (2 * reach + 1) * (ny - 1) + (2 * (half - reach) - 1) * ny + ny // 2
    scratch = [tiles] * (2 * reach)
    scratch += [
        tiles,
        pltpu.VMEM((2, reach + 1, 1, n_amp), jnp.int32),
        pltpu.SMEM((2, reach + 1, 1, n_amp), jnp.int32),
        pltpu.SMEM(slot_of.shape, jnp.int32),
        pltpu.VMEM((n_amp, occ_dev, width), amps.dtype),
        pltpu.VMEM((n_named, occ_dev, width), amps.dtype),
        pltpu.VMEM((n_int,) + integrals.shape, integrals.dtype),
        pltpu.VMEM((n_int,) + amps.shape, amps.dtype),
        pltpu.VMEM((occ_dev, hole_int.shape[1]), hole_int.dtype),
        tiles,
        dma,
        dma((2, reach, n_chunk)),
        dma,
        dma((2, reach)),
        dma((2,)),
        dma,
        dma,
        dma((2,)),
        dma((4, 2)),
        dma((6,)),
    ]
    return pl.pallas_call(
        functools.partial(kernel, n_amp, n_int),
        out_shape=jax.ShapeDtypeStruct(amps.shape, amps.dtype),
        in_specs=[hbm] * len(operands),
        out_specs=pl.BlockSpec(memory_space=pltpu.VMEM),
        scratch_shapes=scratch,
        compiler_params=pltpu.CompilerParams(
            collective_id=0, has_side_effects=True, vmem_limit_bytes=48 * 1024 * 1024
        ),
    )(*(pltpu.with_memory_space_constraint(a, pltpu.HBM) for a in operands))


def solution(mesh):
    in_specs = (
        P("amp", "int", None),
        P("amp", "int", None, None),
        P(),
        P("amp", None, None),
        P("amp", None),
    )
    out_specs = P("amp", "int", None)
    return jax.shard_map(body, mesh=mesh, in_specs=in_specs, out_specs=out_specs, check_vma=False)
```
